32 devices in a mesh: line: 4 (over y, core), tile: 8 (over z, x).
Axes of the slice: x: 2, y: 2, z: 4, core: 2. Of those that a mesh axis runs over, the one named last changes fastest.
Arguments:
- traces: bfloat16 [8, 2048, 128], P('tile', 'line'), may hold values from -6 to 6
- codes: int32 [8, 64], P('tile'), may hold values from 0 to 255
- routes: int32 [4, 128], P('line', 'tile'), may hold values from 0 to 7, as said below
- beam_matrix: bfloat16 [4, 8, 2, 4096, 1024], P('line', 'tile'), may hold values from -0.046875 to 0.046875
- dip_filter: float32 [5, 5], replicated, may hold values from -1 to 1
Outputs:
- migrated: float32 [2, 64, 64, 128], P(None, 'line', 'tile')
The draws below stay inside these ranges and needn't reach their ends.
Inputs may be any that keep to these rules, and one draw needn't show every extreme that they name: `routes`: entry [l, f * 16 + b] is the depth tile that block b of frequency f on line l goes to. Among the 16 entries of one device no tile appears more than 4 times, and in every line some device names one tile exactly 4 times. Among the entries of one line no tile appears more than 32 times, and in every line one tile appears exactly 32 times.
All inputs are finite; a program needn't handle non-finite values.
Results may differ from the reference program's by a relative error of at most 0.004.
Values may be sent and summed in bfloat16 or wider, within the bound.
A program may use at most 64 MiB of HBM per device.

```python
import jax
import jax.numpy as jnp
from jax import lax

S = 64
P_SIZE = 256
WIN = 128
BR = 128
TZ = 8
TX = 128
MAXB = 32
SEND_MOST = 4
F = 8
NB = 16
TRACES = 2048
NZ = 64
N_LINE = 4
N_TILE = 8


def draw_routes(key, part):
    per_owner = MAXB // N_TILE
    spread = N_TILE - 2

    def one_line(line_key):
        key_hot, key_warm, key_rest = jax.random.split(line_key, 3)
        hot_tile = jax.random.randint(key_hot, (), 0, N_TILE)
        offset_warm = jax.random.randint(key_warm, (), 0, N_TILE - 1)
        senders = jnp.arange(N_TILE)
        warm_tiles = (hot_tile + 1 + (senders + offset_warm) % (N_TILE - 1)) % N_TILE

        def one_sender(sender_key, warm_tile):
            key_order, key_blocks = jax.random.split(sender_key)
            shuffled = jax.random.permutation(key_order, N_TILE)
            reserved = ((shuffled == hot_tile) | (shuffled == warm_tile)).astype(jnp.int32)
            spare_tiles = shuffled[jnp.argsort(reserved, stable=True)]
            places = jnp.arange(NB)
            extra_tiles = spare_tiles[jnp.maximum(places - per_owner - SEND_MOST, 0) % spread]
            owners = jnp.where(places < per_owner, hot_tile, jnp.where(places < per_owner + SEND_MOST, warm_tile, extra_tiles))
            return owners[jax.random.permutation(key_blocks, NB)]
        return jax.vmap(one_sender)(jax.random.split(key_rest, N_TILE), warm_tiles).reshape(-1)
    return jax.vmap(one_line)(jax.random.split(key, N_LINE)).astype(jnp.int32)


def plant(drawn, rng, least, high):
    longest = drawn.shape.index(max(drawn.shape))
    spots = []
    for shift in (0, 1):
        where = [jax.random.randint(jax.random.fold_in(rng, axis), (), 0, length) for axis, length in enumerate(drawn.shape)]
        where[longest] = (where[longest] + shift) % drawn.shape[longest]
        spots.append(tuple(where))
    return drawn.at[spots[0]].set(least).at[spots[1]].set(high)


def level_of(key, shape, shards, least, largest):
    loudness = 1.0
    for axis_at, parts in shards:
        heights = jax.random.uniform(jax.random.fold_in(jax.random.fold_in(key, 6), axis_at), (parts,), jnp.float32, least / len(shards), largest / len(shards))
        loudness = loudness * jnp.repeat(jnp.exp(heights), shape[axis_at] // parts).reshape((-1,) + (1,) * (len(shape) - 1 - axis_at))
    return loudness


def bell_draw(rng, dims, deviation, limit, pieces=(), held_as=jnp.bfloat16):
    level = level_of(rng, dims, pieces, -0.22, 0.18) if pieces else 1.0
    entries = jax.random.normal(rng, dims, jnp.float32) * deviation * level
    return jnp.minimum(jnp.maximum(entries, -limit), limit).astype(held_as)


def setup_inputs(seed: int = 0) -> dict:
    key_of = jax.random.split(jax.random.key(seed), 6)
    traces = bell_draw(key_of[0], (F, TRACES, 2 * S), 1.0, 6.0, ((0, 8), (1, 4)))
    codes = plant(jax.random.randint(key_of[1], (F, S), 0, 256), jax.random.fold_in(key_of[1], 1), 0, 255).astype(jnp.int32)
    routes = draw_routes(jax.random.fold_in(key_of[5], 71), 0)
    beam_matrix = bell_draw(key_of[3], (N_LINE, N_TILE, 2, MAXB * BR, TZ * TX), (4 * MAXB * BR) ** -0.5, 0.046875, ((0, 4), (1, 8)))
    dip_filter = bell_draw(key_of[4], (5, 5), 0.2, 1.0, (), jnp.float32)
    return dict(traces=traces, codes=codes, routes=routes, beam_matrix=beam_matrix, dip_filter=dip_filter)


def slant_table(frequency, freq_count):
    slopes = jnp.arange(P_SIZE, dtype=jnp.float32) - P_SIZE / 2
    offsets = jnp.arange(WIN, dtype=jnp.float32) - (WIN - 1) / 2
    factor = 2.0 + frequency.astype(jnp.float32) / freq_count
    phase_angle = jnp.pi * factor * slopes[:, None] * offsets[None, :] / WIN
    taper_row = jnp.exp(-0.5 * (offsets / (0.4 * WIN)) ** 2)
    taper_row = taper_row / jnp.sqrt(jnp.sum(taper_row * taper_row))
    return jnp.concatenate([taper_row * jnp.cos(phase_angle), -taper_row * jnp.sin(phase_angle)], 0).astype(jnp.bfloat16)

def rotate(stacked, code_row):
    real_part = stacked[..., :P_SIZE, :S] - stacked[..., P_SIZE:, S:]
    imag_part = stacked[..., :P_SIZE, S:] + stacked[..., P_SIZE:, :S]
    code_angle = 2.0 * jnp.pi * code_row.astype(jnp.float32) / 256.0
    cosine = jnp.cos(code_angle)
    sine_part = jnp.sin(code_angle)
    return jnp.concatenate([real_part * cosine + imag_part * sine_part, imag_part * cosine - real_part * sine_part], -1).astype(jnp.bfloat16)

def dip_apply(padded, dip_filter):
    depth_rows = padded.shape[2] - 4
    widened = jnp.pad(padded, ((0, 0), (0, 0), (0, 0), (2, 2)))
    result = jnp.zeros(padded.shape[:2] + (depth_rows, TX), jnp.float32)
    for down_step in range(5):
        for side_step in range(5):
            result = result + dip_filter[down_step, side_step] * widened[:, :, down_step:down_step + depth_rows, side_step:side_step + TX]
    return result

def reference(traces, codes, routes, beam_matrix, dip_filter):
    tables = jax.vmap(lambda frequency: slant_table(frequency, F))(jnp.arange(F))
    half_win = WIN // 2
    extended = jnp.concatenate([traces, jnp.zeros((F, half_win, 2 * S), traces.dtype)], 1)
    halves = extended.reshape(F, -1, half_win, 2 * S)
    windows = jnp.concatenate([halves[:, :-1], halves[:, 1:]], 2)
    stacked = jnp.einsum('fpj,fmjc->fmpc', tables.astype(jnp.float32), windows.astype(jnp.float32), precision=lax.Precision.HIGHEST)
    beam_rows = rotate(stacked, codes[:, None, None, :])
    blocks = beam_rows.reshape(F, N_LINE, NB, BR * 2 * S)
    per_line = jnp.transpose(blocks, (1, 0, 2, 3)).reshape(N_LINE, F * NB, BR * 2 * S)

    def tile_image(tile_id):

        def add_line(total, line_id):
            is_mine = (routes[line_id] == tile_id).astype(jnp.int32)
            slot_ids = jnp.where(is_mine > 0, jnp.cumsum(is_mine) - 1, MAXB).astype(jnp.int32)
            compact = jnp.zeros((MAXB, BR * 2 * S), jnp.bfloat16).at[slot_ids].set(per_line[line_id], mode='drop')
            slot_rows = compact.reshape(MAXB * BR, 2 * S)
            matrices = beam_matrix[line_id, tile_id]
            with_real = jnp.dot(slot_rows.T, matrices[0], preferred_element_type=jnp.float32)
            with_imag = jnp.dot(slot_rows.T, matrices[1], preferred_element_type=jnp.float32)
            image_re = with_real[:S] - with_imag[S:]
            image_im = with_real[S:] + with_imag[:S]
            return (total + jnp.stack([image_re, image_im]), None)
        total, ignored = lax.scan(add_line, jnp.zeros((2, S, TZ * TX), jnp.float32), jnp.arange(N_LINE))
        return total
    images = lax.map(tile_image, jnp.arange(N_TILE))
    image_all = images.reshape(N_TILE, 2, S, TZ, TX).transpose(1, 2, 0, 3, 4).reshape(2, S, NZ, TX)
    padded = jnp.pad(image_all, ((0, 0), (0, 0), (2, 2), (0, 0)))
    return dip_apply(padded, dip_filter)
```

```python
import jax
import jax.numpy as jnp
from jax import lax
from jax.sharding import PartitionSpec as P

S = 64
P_SIZE = 256
WIN = 128
BR = 128
TZ = 8
TX = 128
MAXB = 32
SEND_MOST = 4


def passed_along(value, axis, steps):
    count = lax.axis_size(axis)
    first, last = (max(0, -steps), min(count, count - steps))
    return lax.ppermute(value, axis, [(source, source + steps) for source in range(first, last)])


def with_halo(cells, sides, width):
    for axis, dim in sides:
        count = lax.axis_size(axis)
        ends = count - 1
        head = lax.slice_in_dim(cells, 0, width, axis=dim)
        tail = lax.slice_in_dim(cells, cells.shape[dim] - width, cells.shape[dim], axis=dim)
        cells = jnp.concatenate(
            [
                lax.ppermute(tail, axis, [(i, (i + 1) % count) for i in range(ends)]),
                cells,
                lax.ppermute(head, axis, [((i + 1) % count, i) for i in range(ends)]),
            ],
            axis=dim,
        )
    return cells


def slant_table(frequency, freq_count):
    slopes = jnp.arange(P_SIZE, dtype=jnp.float32) - P_SIZE / 2
    offsets = jnp.arange(WIN, dtype=jnp.float32) - (WIN - 1) / 2
    factor = 2.0 + frequency.astype(jnp.float32) / freq_count
    phase_angle = jnp.pi * factor * slopes[:, None] * offsets[None, :] / WIN
    taper_row = jnp.exp(-0.5 * (offsets / (0.4 * WIN)) ** 2)
    taper_row = taper_row / jnp.sqrt(jnp.sum(taper_row * taper_row))
    return jnp.concatenate(
        [taper_row * jnp.cos(phase_angle), -taper_row * jnp.sin(phase_angle)], 0
    ).astype(jnp.bfloat16)


def rotate(stacked, code_row):
    real_part = stacked[..., :P_SIZE, :S] - stacked[..., P_SIZE:, S:]
    imag_part = stacked[..., :P_SIZE, S:] + stacked[..., P_SIZE:, :S]
    code_angle = 2.0 * jnp.pi * code_row.astype(jnp.float32) / 256.0
    cosine = jnp.cos(code_angle)
    sine_part = jnp.sin(code_angle)
    return jnp.concatenate(
        [real_part * cosine + imag_part * sine_part, imag_part * cosine - real_part * sine_part], -1
    ).astype(jnp.bfloat16)


def dip_apply(padded, dip_filter):
    depth_rows = padded.shape[2] - 4
    widened = jnp.pad(padded, ((0, 0), (0, 0), (0, 0), (2, 2)))
    result = jnp.zeros(padded.shape[:2] + (depth_rows, TX), jnp.float32)
    for down_step in range(5):
        for side_step in range(5):
            result = (
                result
                + dip_filter[down_step, side_step]
                * widened[:, :, down_step : down_step + depth_rows, side_step : side_step + TX]
            )
    return result


def per_device(traces, codes, routes, beam_matrix, dip_filter):
    tile_count = lax.axis_size("tile")
    my_tile = lax.axis_index("tile")
    half_win = WIN // 2
    row_width = BR * 2 * S
    local_traces = traces[0]
    next_rim = passed_along(local_traces[:half_win], "line", -1)
    extended = jnp.concatenate([local_traces, next_rim], 0)
    halves = extended.reshape(-1, half_win, 2 * S)
    windows = jnp.concatenate([halves[:-1], halves[1:]], 1)
    table_now = slant_table(my_tile, tile_count)
    stacked = jnp.einsum("pj,wjc->wpc", table_now, windows, preferred_element_type=jnp.float32)
    beam_rows = rotate(stacked, codes[0])
    blocks = beam_rows.reshape(-1, row_width)
    route_row = routes[0]
    peer_ids = jnp.arange(tile_count)
    member = (route_row[:, None] == peer_ids[None, :]).astype(jnp.int32)
    places = jnp.arange(member.shape[0])
    earlier = (places[None, :] < places[:, None]).astype(jnp.int32)
    before = jnp.sum(earlier[:, :, None] * member[None, :, :], 1)
    rank_in = jnp.sum(before * member, 1)
    send_slot = route_row * SEND_MOST + rank_in
    picker = (jnp.arange(tile_count * SEND_MOST)[:, None] == send_slot[None, :]).astype(
        jnp.bfloat16
    )
    outgoing = jnp.dot(picker, blocks, preferred_element_type=jnp.float32).astype(jnp.bfloat16)
    outgoing = outgoing.reshape(tile_count, SEND_MOST, row_width)
    sent_counts = jnp.sum(member, 0)[:, None]
    incoming, got_counts = (
        lax.all_to_all(outgoing, "tile", split_axis=0, concat_axis=0, tiled=True),
        lax.all_to_all(sent_counts, "tile", split_axis=0, concat_axis=0, tiled=True),
    )
    arrived = got_counts[:, 0]
    first_slot = jnp.sum(jnp.where(peer_ids[None, :] < peer_ids[:, None], arrived[None, :], 0), 1)
    rank_list = jnp.arange(SEND_MOST)
    slot_ids = jnp.where(
        rank_list[None, :] < arrived[:, None], first_slot[:, None] + rank_list[None, :], MAXB
    ).reshape(-1)
    placer = (jnp.arange(MAXB)[:, None] == slot_ids[None, :]).astype(jnp.bfloat16)
    compact = jnp.dot(
        placer, incoming.reshape(-1, row_width), preferred_element_type=jnp.float32
    ).astype(jnp.bfloat16)
    matrices = beam_matrix[0, 0]
    slot_rows = compact.reshape(MAXB * BR, 2 * S)
    contract_dims = (((0,), (0,)), ((), ()))
    with_real = lax.dot_general(
        slot_rows, matrices[0], contract_dims, preferred_element_type=jnp.float32
    )
    with_imag = lax.dot_general(
        slot_rows, matrices[1], contract_dims, preferred_element_type=jnp.float32
    )
    image_re = with_real[:S] - with_imag[S:]
    image_im = with_real[S:] + with_imag[:S]
    partial_image = jnp.stack([image_re, image_im]).reshape(2, S, TZ, TX)
    summed = lax.psum_scatter(partial_image, "line", scatter_dimension=1, tiled=True)
    rimmed = with_halo(summed, (("tile", 2),), 2)
    return dip_apply(rimmed, dip_filter)


def solution(mesh):
    in_specs = (
        P("tile", "line", None),
        P("tile", None),
        P("line", "tile"),
        P("line", "tile", None, None, None),
        P(),
    )
    out_specs = P(None, "line", "tile", None)
    return jax.shard_map(
        per_device, mesh=mesh, in_specs=in_specs, out_specs=out_specs, check_vma=False
    )
```

```python
import functools

import jax
import jax.numpy as jnp
import numpy as np
from jax import lax
from jax.experimental import pallas as pl
from jax.experimental.pallas import tpu as pltpu
from jax.sharding import PartitionSpec as P

P_SIZE = 256
WIN = 128
BR = 128
LANES = 128
CW = 256
MESH = pl.DeviceIdType.MESH


def slant_tables(freq_count):
    f32 = np.float32
    slopes = np.arange(P_SIZE, dtype=f32) - f32(P_SIZE / 2)
    offsets = np.arange(WIN, dtype=f32) - f32((WIN - 1) / 2)
    taper = np.exp(f32(-0.5) * (offsets / f32(0.4 * WIN)) ** 2)
    taper = taper / np.sqrt(np.sum(taper * taper))
    out = np.zeros((freq_count, 2, P_SIZE // BR, 2 * WIN, BR), f32)
    for f in range(freq_count):
        factor = f32(2.0) + f32(f) / f32(freq_count)
        angle = f32(np.pi) * factor * slopes[:, None] * offsets[None, :] / f32(WIN)
        re, im = taper * np.cos(angle), -taper * np.sin(angle)
        for odd in range(2):
            shift = odd * (WIN // 2)
            both = np.concatenate([np.roll(re, shift, 1), np.roll(im, shift, 1)], 1)
            for q in range(P_SIZE // BR):
                out[f, odd, q] = both[q * BR : (q + 1) * BR].T
    return out.reshape(-1, 2 * WIN, BR)


def kernel(
    n_line, n_tile, n_block, n_slot, n_shot,
    traces, codes, routes, dip, table_hbm, beam_hbm, out,
    tiles, halo, meta, table, beam, slots_v, slots, cosine, sine, stacked, part, r_main, r_top, r_bot,
    local, main_send, main_recv, halo_send, halo_recv, head_send, head_recv, meta_send, meta_recv,
    part_send, part_recv, top_send, top_recv, bot_send, bot_recv,
):
    line, tile = lax.axis_index("line"), lax.axis_index("tile")
    n_z = n_tile // 2
    z, x = tile // 2, tile % 2
    half = WIN // 2
    n_full = traces.shape[0] // LANES
    shots = n_shot // n_line
    depth = n_slot * BR
    pieces = out.shape[1] * LANES // CW

    fetches = [pltpu.make_async_copy(table_hbm, table, local.at[0])]
    for i in range(4):
        rows = pl.ds(i * (2 * depth // 4), 2 * depth // 4)
        fetches.append(pltpu.make_async_copy(beam_hbm.at[rows], beam.at[rows], local.at[1 + i]))
    for fetch in fetches:
        fetch.start()

    barrier = pltpu.get_barrier_semaphore()

    def greet(to_line, to_tile):
        pl.semaphore_signal(barrier, inc=1, device_id=(to_line, to_tile), device_id_type=MESH)

    for k in range(1, n_tile):
        greet(line, lax.rem(tile + k, n_tile))
    for k in range(1, n_line):
        other = lax.rem(line + k, n_line)
        greet(other, tile)

        @pl.when(tile > 0)
        def _():
            greet(other, tile - 1)

        @pl.when(tile < n_tile - 1)
        def _():
            greet(other, tile + 1)

    for i in range(n_full):
        tiles[tile, i] = jnp.transpose(traces[i * LANES : (i + 1) * LANES, :])
    meta[tile] = jnp.zeros((8, LANES), jnp.int32)
    meta[tile, 0:1, 0:n_block] = routes[...]
    meta[tile, 1:2, 0:n_shot] = codes[...]
    meta[tile, 1:2, n_shot : 2 * n_shot] = codes[...]

    @pl.when(line == n_line - 1)
    def _():
        halo[tile] = jnp.zeros((half, LANES), jnp.bfloat16)

    @pl.when(tile == 0)
    def _():
        r_top[...] = jnp.zeros_like(r_top)

    @pl.when(tile == n_tile - 1)
    def _():
        r_bot[...] = jnp.zeros_like(r_bot)

    greeted = n_tile - 1 + (n_line - 1) * (
        1 + (tile > 0).astype(jnp.int32) + (tile < n_tile - 1).astype(jnp.int32)
    )
    pl.semaphore_wait(barrier, greeted)

    def remote(src, dst, send, recv, to_line, to_tile):
        return pltpu.make_async_remote_copy(
            src_ref=src, dst_ref=dst, send_sem=send, recv_sem=recv,
            device_id=(to_line, to_tile), device_id_type=MESH,
        )

    def main_copy(source, way, to_tile):
        block = tiles.at[source, pl.ds(0, n_full)]
        return remote(block, block, main_send.at[source, way], main_recv.at[source], line, to_tile)

    def halo_copy(source, way, to_tile):
        block = halo.at[source]
        return remote(block, block, halo_send.at[source, way], halo_recv.at[source], line, to_tile)

    across = z * 2 + 1 - x
    head_out = remote(
        traces.at[pl.ds(0, half)], halo.at[tile], head_send, head_recv, jnp.maximum(line - 1, 0), tile
    )
    meta_out = [
        remote(meta.at[tile], meta.at[tile], meta_send.at[k], meta_recv.at[tile], line, lax.rem(tile + k, n_tile))
        for k in range(1, n_tile)
    ]

    def onward(copy, step, way, act):
        come_from = z - step * way
        source = come_from * 2 + x

        @pl.when((come_from >= 0) & (come_from < n_z))
        def _():
            if act == "start" and step:
                copy(source, 0, across).wait_recv()
            for slot, to in ((0, 1), (1, -1)):
                if step and to != way:
                    continue

                @pl.when((z + to >= 0) & (z + to < n_z))
                def _():
                    c = copy(source, slot, (z + to) * 2 + x)
                    c.start() if act == "start" else c.wait_send()

            c = copy(source, 2, across)
            c.start() if act == "start" else c.wait_send()

    @pl.when(line > 0)
    def _():
        head_out.start()

    for c in meta_out:
        c.start()
    onward(main_copy, 0, 1, "start")

    @pl.when(line < n_line - 1)
    def _():
        head_out.wait_recv()

    onward(halo_copy, 0, 1, "start")

    for k in range(1, n_tile):
        source = lax.rem(tile + k, n_tile)
        remote(meta.at[source], meta.at[source], meta_send.at[k], meta_recv.at[source], line, source).wait_recv()
    lane_row = lax.broadcasted_iota(jnp.int32, (8, LANES), 1)
    wanted = lax.broadcasted_iota(jnp.int32, (n_slot, LANES), 0)
    lane_slots = lax.broadcasted_iota(jnp.int32, (n_slot, LANES), 1)
    found = jnp.zeros((n_slot, LANES), jnp.int32)
    before = jnp.zeros((1, 1), jnp.int32)
    for f in range(n_tile):
        row = meta[f]
        member = jnp.where((lane_row < n_block) & (row == tile), 1, 0)
        upto = member
        step = 1
        while step < n_block:
            upto = upto + jnp.where(lane_row >= step, pltpu.roll(upto, step, 1), 0)
            step *= 2
        rank = jnp.where(member > 0, upto - member + before, -1)
        found = found + jnp.where(
            jnp.broadcast_to(rank[0:1], (n_slot, LANES)) == wanted, lane_slots + (f * n_block + 1), 0
        )
        before = before + jnp.sum(member[0:1], axis=1, keepdims=True)
        angle = 2.0 * jnp.pi * row[1:2].astype(jnp.float32) / 256.0
        upright = jnp.transpose(jnp.broadcast_to(angle, (LANES, LANES)))
        sign = jnp.where(lax.broadcasted_iota(jnp.int32, (LANES, LANES), 0) < n_shot, 1.0, -1.0)
        cosine[f] = upright
        sine[f] = sign
    slots_v[...] = jnp.broadcast_to(jnp.sum(found, axis=1, keepdims=True), (n_slot, LANES))
    to_scalars = pltpu.make_async_copy(slots_v, slots, local.at[5])
    to_scalars.start()

    for step in range(1, n_z):
        for way in (1, -1):
            onward(main_copy, step, way, "start")
        for way in (1, -1):
            onward(halo_copy, step, way, "start")

    def phases(f, carry):
        angle = cosine[f]
        sine[f] = sine[f] * jnp.sin(angle)
        cosine[f] = jnp.cos(angle)
        return carry

    lax.fori_loop(0, n_tile, phases, 0)

    for place in range(n_z):
        source = place * 2 + 1 - x
        main_copy(source, 0, across).wait_recv()
        halo_copy(source, 0, across).wait_recv()
    for f in range(n_tile):
        rim = jnp.concatenate([halo[f], jnp.zeros((LANES - half, LANES), jnp.bfloat16)], 0)
        tiles[f, n_full] = jnp.transpose(rim)
    to_scalars.wait()
    fetches[0].wait()

    first_half = lax.broadcasted_iota(jnp.int32, (LANES, LANES), 1) < half

    def swapped(value):
        return jnp.concatenate([value[n_shot:], value[:n_shot]], 0)

    def turned(value):
        return jnp.concatenate([-value[n_shot:], value[:n_shot]], 0)

    def one_slot(n, carry):
        name = slots[n, 0]
        there = jnp.where(name > 0, 1.0, 0.0)
        block = jnp.maximum(name - 1, 0)
        f = block // n_block
        b = block - f * n_block
        window = b // 2
        data = jnp.where(first_half, tiles[f, (window + 1) // 2], tiles[f, window // 2])
        lhs = jnp.concatenate([data, turned(data)], 1)
        raw = jnp.dot(lhs, table[f * 4 + b % 4], preferred_element_type=jnp.float32)
        beam_now = ((raw * cosine[f] + swapped(raw) * sine[f]) * there)
        at = pl.multiple_of(n * BR, BR)
        stacked[:, pl.ds(at, BR)] = beam_now.astype(jnp.bfloat16)
        stacked[:, pl.ds(pl.multiple_of(at + depth, BR), BR)] = turned(beam_now).astype(jnp.bfloat16)
        return carry

    lax.fori_loop(0, n_slot, one_slot, 0)

    for fetch in fetches[1:]:
        fetch.wait()

    def piece_copy(k, j):
        to = lax.rem(line + k, n_line)
        cols = pl.ds(j * CW, CW)
        return remote(
            part.at[to, :, cols], r_main.at[k - 1, :, cols], part_send.at[k - 1, j], part_recv.at[k - 1, j], to, tile
        )

    def edge_copy(k, up):
        to = lax.rem(line + k, n_line)
        if up:
            return remote(
                part.at[to, :, pl.ds(0, CW)], r_bot.at[k], top_send.at[k], bot_recv.at[k], to,
                jnp.maximum(tile - 1, 0),
            )
        return remote(
            part.at[to, :, pl.ds((pieces - 1) * CW, CW)], r_top.at[k], bot_send.at[k], top_recv.at[k], to,
            jnp.minimum(tile + 1, n_tile - 1),
        )

    for j in [0, pieces - 1, *range(1, pieces - 1)]:
        image = jnp.dot(stacked[...], beam[:, j * CW : (j + 1) * CW], preferred_element_type=jnp.float32)
        for to in range(n_line):
            low = to * shots
            part[to, :, j * CW : (j + 1) * CW] = jnp.concatenate(
                [image[low : low + shots], image[n_shot + low : n_shot + low + shots]], 0
            ).astype(jnp.bfloat16)
        if j == 0:

            @pl.when(tile > 0)
            def _():
                for k in range(n_line):
                    edge_copy(k, True).start()

        if j == pieces - 1:

            @pl.when(tile < n_tile - 1)
            def _():
                for k in range(n_line):
                    edge_copy(k, False).start()

        for k in range(1, n_line):
            piece_copy(k, j).start()

    @pl.when(line > 0)
    def _():
        head_out.wait_send()

    for c in meta_out:
        c.wait_send()
    for copy in (main_copy, halo_copy):
        onward(copy, 0, 1, "wait")
        for step in range(1, n_z):
            for way in (1, -1):
                onward(copy, step, way, "wait")

    @pl.when(tile > 0)
    def _():
        for k in range(n_line):
            edge_copy(k, False).wait_recv()
            edge_copy(k, True).wait_send()

    @pl.when(tile < n_tile - 1)
    def _():
        for k in range(n_line):
            edge_copy(k, True).wait_recv()
            edge_copy(k, False).wait_send()

    for j in range(pieces):
        for k in range(1, n_line):
            piece_copy(k, j).wait()

    wide = jnp.float32
    image_rows = []
    top = sum(r_top[k].astype(wide) for k in range(n_line))
    bottom = sum(r_bot[k].astype(wide) for k in range(n_line))
    image_rows += [top[:, :LANES], top[:, LANES:]]
    for row in range(out.shape[1]):
        cols = slice(row * LANES, (row + 1) * LANES)
        total = part[line, :, cols].astype(wide)
        for k in range(n_line - 1):
            total = total + r_main[k, :, cols].astype(wide)
        image_rows.append(total)
    image_rows += [bottom[:, :LANES], bottom[:, LANES:]]
    lane = lax.broadcasted_iota(jnp.int32, image_rows[0].shape, 1)
    for row in range(out.shape[1]):
        result = None
        for side in range(5):
            column = sum(dip[down, side] * image_rows[row + down] for down in range(5))
            move = side - 2
            if move:
                column = pltpu.roll(column, (-move) % LANES, 1)
                column = jnp.where((lane + move >= 0) & (lane + move < LANES), column, 0.0)
            result = column if result is None else result + column
        out[:, row, :] = result


def per_device(traces, codes, routes, beam_matrix, dip_filter):
    n_line, n_tile = lax.axis_size("line"), lax.axis_size("tile")
    n_shot = codes.shape[1]
    n_block = routes.shape[1]
    depth, pixels = beam_matrix.shape[3:]
    n_slot = depth // BR
    n_full = traces.shape[1] // LANES
    rows = 2 * (n_shot // n_line)
    tall = pixels // LANES
    pieces = pixels // CW
    table = jnp.asarray(slant_tables(n_tile)).astype(jnp.bfloat16)
    bf16, f32, i32 = jnp.bfloat16, jnp.float32, jnp.int32
    dma = pltpu.SemaphoreType.DMA
    vmem = pl.BlockSpec(memory_space=pltpu.VMEM)
    hbm = pl.BlockSpec(memory_space=pl.ANY)
    result = pl.pallas_call(
        functools.partial(kernel, n_line, n_tile, n_block, n_slot, n_shot),
        out_shape=jax.ShapeDtypeStruct((rows, tall, LANES), f32),
        in_specs=[vmem, vmem, vmem, pl.BlockSpec(memory_space=pltpu.SMEM), hbm, hbm],
        out_specs=vmem,
        scratch_shapes=[
            pltpu.VMEM((n_tile, n_full + 1, LANES, LANES), bf16),
            pltpu.VMEM((n_tile, WIN // 2, LANES), bf16),
            pltpu.VMEM((n_tile, 8, LANES), i32),
            pltpu.VMEM(table.shape, bf16),
            pltpu.VMEM((2 * depth, pixels), bf16),
            pltpu.VMEM((n_slot, LANES), i32),
            pltpu.SMEM((n_slot, LANES), i32),
            pltpu.VMEM((n_tile, LANES, LANES), f32),
            pltpu.VMEM((n_tile, LANES, LANES), f32),
            pltpu.VMEM((2 * n_shot, 2 * depth), bf16),
            pltpu.VMEM((n_line, rows, pixels), bf16),
            pltpu.VMEM((n_line - 1, rows, pixels), bf16),
            pltpu.VMEM((n_line, rows, CW), bf16),
            pltpu.VMEM((n_line, rows, CW), bf16),
            dma((6,)),
            dma((n_tile, 3)), dma((n_tile,)),
            dma((n_tile, 3)), dma((n_tile,)),
            dma, dma,
            dma((n_tile,)), dma((n_tile,)),
            dma((n_line - 1, pieces)), dma((n_line - 1, pieces)),
            dma((n_line,)), dma((n_line,)),
            dma((n_line,)), dma((n_line,)),
        ],
        compiler_params=pltpu.CompilerParams(
            collective_id=0, has_side_effects=True, vmem_limit_bytes=50 * 2**20
        ),
    )(traces[0], codes, routes, dip_filter, table, beam_matrix.reshape(2 * depth, pixels))
    return result.reshape(2, rows // 2, tall, LANES)


def solution(mesh):
    in_specs = (
        P("tile", "line", None),
        P("tile", None),
        P("line", "tile"),
        P("line", "tile", None, None, None),
        P(),
    )
    out_specs = P(None, "line", "tile", None)
    return jax.shard_map(
        per_device, mesh=mesh, in_specs=in_specs, out_specs=out_specs, check_vma=False
    )
```

```python
import functools

import jax
import jax.numpy as jnp
import numpy as np
from jax import lax
from jax.experimental import pallas as pl
from jax.experimental.pallas import tpu as pltpu
from jax.sharding import PartitionSpec as P

P_SIZE = 256
WIN = 128
BR = 128
LANES = 128
CW = 256
MESH = pl.DeviceIdType.MESH


def slant_tables(freq_count):
    f32 = np.float32
    slopes = np.arange(P_SIZE, dtype=f32) - f32(P_SIZE / 2)
    offsets = np.arange(WIN, dtype=f32) - f32((WIN - 1) / 2)
    taper = np.exp(f32(-0.5) * (offsets / f32(0.4 * WIN)) ** 2)
    taper = taper / np.sqrt(np.sum(taper * taper))
    out = np.zeros((freq_count, 2, P_SIZE // BR, 2 * WIN, BR), f32)
    for f in range(freq_count):
        factor = f32(2.0) + f32(f) / f32(freq_count)
        angle = f32(np.pi) * factor * slopes[:, None] * offsets[None, :] / f32(WIN)
        re, im = taper * np.cos(angle), -taper * np.sin(angle)
        for odd in range(2):
            shift = odd * (WIN // 2)
            both = np.concatenate([np.roll(re, shift, 1), np.roll(im, shift, 1)], 1)
            for q in range(P_SIZE // BR):
                out[f, odd, q] = both[q * BR : (q + 1) * BR].T
    return out.reshape(-1, 2 * WIN, BR)


def kernel(
    n_line, n_tile, n_block, n_slot, n_shot,
    traces_hbm, codes, routes, dip, table_hbm, beam_hbm, out,
    traces, tiles, halo, meta, table, beam, slots_v, slots, cosine, sine, stacked, part, r_main, r_top, r_bot,
    local, main_send, main_recv, halo_send, halo_recv, head_send, head_recv, meta_send, meta_recv,
    part_send, part_recv, top_send, top_recv, bot_send, bot_recv,
):
    line, tile = lax.axis_index("line"), lax.axis_index("tile")
    n_z = n_tile // 2
    z, x = tile // 2, tile % 2
    half = WIN // 2
    n_full = traces.shape[0] // LANES
    shots = n_shot // n_line
    depth = n_slot * BR
    pieces = out.shape[1] * LANES // CW

    own_fetch = pltpu.make_async_copy(traces_hbm, traces, local.at[6])
    own_fetch.start()
    fetches = [pltpu.make_async_copy(table_hbm, table, local.at[0])]
    for i in range(4):
        rows = pl.ds(i * (2 * depth // 4), 2 * depth // 4)
        fetches.append(pltpu.make_async_copy(beam_hbm.at[rows], beam.at[rows], local.at[1 + i]))
    for fetch in fetches:
        fetch.start()

    barrier = pltpu.get_barrier_semaphore()

    def greet(to_line, to_tile):
        pl.semaphore_signal(barrier, inc=1, device_id=(to_line, to_tile), device_id_type=MESH)

    for k in range(1, n_tile):
        greet(line, lax.rem(tile + k, n_tile))
    for k in range(1, n_line):
        other = lax.rem(line + k, n_line)
        greet(other, tile)

        @pl.when(tile > 0)
        def _():
            greet(other, tile - 1)

        @pl.when(tile < n_tile - 1)
        def _():
            greet(other, tile + 1)

    own_fetch.wait()
    for i in range(n_full):
        tiles[tile, i] = jnp.transpose(traces[i * LANES : (i + 1) * LANES, :])
    meta[tile] = jnp.zeros((8, LANES), jnp.int32)
    meta[tile, 0:1, 0:n_block] = routes[...]
    meta[tile, 1:2, 0:n_shot] = codes[...]
    meta[tile, 1:2, n_shot : 2 * n_shot] = codes[...]

    @pl.when(line == n_line - 1)
    def _():
        halo[tile] = jnp.zeros((half, LANES), jnp.bfloat16)

    @pl.when(tile == 0)
    def _():
        r_top[...] = jnp.zeros_like(r_top)

    @pl.when(tile == n_tile - 1)
    def _():
        r_bot[...] = jnp.zeros_like(r_bot)

    greeted = n_tile - 1 + (n_line - 1) * (
        1 + (tile > 0).astype(jnp.int32) + (tile < n_tile - 1).astype(jnp.int32)
    )
    pl.semaphore_wait(barrier, greeted)

    def remote(src, dst, send, recv, to_line, to_tile):
        return pltpu.make_async_remote_copy(
            src_ref=src, dst_ref=dst, send_sem=send, recv_sem=recv,
            device_id=(to_line, to_tile), device_id_type=MESH,
        )

    def main_piece(piece):
        def main_copy(source, way, to_tile):
            block = tiles.at[source, pl.ds(piece * (n_full // 2), n_full // 2)]
            at = source * 2 + piece
            return remote(block, block, main_send.at[at, way], main_recv.at[at], line, to_tile)

        return main_copy

    mains = [main_piece(0), main_piece(1)]

    def halo_copy(source, way, to_tile):
        block = halo.at[source]
        return remote(block, block, halo_send.at[source, way], halo_recv.at[source], line, to_tile)

    across = z * 2 + 1 - x
    head_out = remote(
        traces.at[pl.ds(0, half)], halo.at[tile], head_send, head_recv, jnp.maximum(line - 1, 0), tile
    )
    meta_out = [
        remote(meta.at[tile], meta.at[tile], meta_send.at[k], meta_recv.at[tile], line, lax.rem(tile + k, n_tile))
        for k in range(1, n_tile)
    ]

    distances = [(step, way) for step in range(1, n_z) for way in (1, -1)]

    def along(copy, source, way, act):
        @pl.when((z + way >= 0) & (z + way < n_z))
        def _():
            act(copy(source, 1 if way > 0 else 2, (z + way) * 2 + x))

    def own(copy, act):
        along(copy, tile, 1, act)
        along(copy, tile, -1, act)
        act(copy(tile, 0, across))

    def onward(copy, step, way, act, arrive=False):
        come_from = z - step * way
        source = come_from * 2 + x

        @pl.when((come_from >= 0) & (come_from < n_z))
        def _():
            if arrive:
                copy(source, 0, across).wait_recv()
            along(copy, source, way, act)
            act(copy(source, 0, across))

    @pl.when(line > 0)
    def _():
        head_out.start()

    for c in meta_out:
        c.start()
    for copy in mains:
        own(copy, lambda c: c.start())

    @pl.when(line < n_line - 1)
    def _():
        head_out.wait_recv()

    own(halo_copy, lambda c: c.start())

    for k in range(1, n_tile):
        source = lax.rem(tile + k, n_tile)
        remote(meta.at[source], meta.at[source], meta_send.at[k], meta_recv.at[source], line, source).wait_recv()
    lane_row = lax.broadcasted_iota(jnp.int32, (8, LANES), 1)
    wanted = lax.broadcasted_iota(jnp.int32, (n_slot, LANES), 0)
    lane_slots = lax.broadcasted_iota(jnp.int32, (n_slot, LANES), 1)
    found = jnp.zeros((n_slot, LANES), jnp.int32)
    before = jnp.zeros((1, 1), jnp.int32)
    for f in range(n_tile):
        row = meta[f]
        member = jnp.where((lane_row < n_block) & (row == tile), 1, 0)
        upto = member
        step = 1
        while step < n_block:
            upto = upto + jnp.where(lane_row >= step, pltpu.roll(upto, step, 1), 0)
            step *= 2
        rank = jnp.where(member > 0, upto - member + before, -1)
        found = found + jnp.where(
            jnp.broadcast_to(rank[0:1], (n_slot, LANES)) == wanted, lane_slots + (f * n_block + 1), 0
        )
        before = before + jnp.sum(member[0:1], axis=1, keepdims=True)
    slots_v[...] = jnp.broadcast_to(jnp.sum(found, axis=1, keepdims=True), (n_slot, LANES))
    to_scalars = pltpu.make_async_copy(slots_v, slots, local.at[5])
    to_scalars.start()

    for step, way in distances:
        for copy in mains:
            onward(copy, step, way, lambda c: c.start(), True)
    for step, way in distances:
        onward(halo_copy, step, way, lambda c: c.start(), True)

    code_rows = jnp.concatenate([meta[f, 1:2] for f in range(n_tile)], 0)
    angle = 2.0 * jnp.pi * code_rows.astype(jnp.float32) / 256.0
    sign = jnp.where(lax.broadcasted_iota(jnp.int32, angle.shape, 1) < n_shot, 1.0, -1.0)
    for into, row in ((cosine, jnp.cos(angle)), (sine, jnp.sin(angle) * sign)):
        columns = jnp.transpose(jnp.concatenate([row, jnp.zeros((LANES - n_tile, LANES), jnp.float32)], 0))
        for f in range(n_tile):
            into[f] = jnp.broadcast_to(columns[:, f : f + 1], (LANES, LANES))

    for place in range(n_z):
        source = place * 2 + 1 - x
        for copy in mains:
            copy(source, 0, across).wait_recv()
        halo_copy(source, 0, across).wait_recv()
    for f in range(n_tile):
        rim = jnp.concatenate([halo[f], jnp.zeros((LANES - half, LANES), jnp.bfloat16)], 0)
        tiles[f, n_full] = jnp.transpose(rim)
    to_scalars.wait()
    fetches[0].wait()

    first_half = lax.broadcasted_iota(jnp.int32, (LANES, LANES), 1) < half

    def swapped(value):
        return jnp.concatenate([value[n_shot:], value[:n_shot]], 0)

    def turned(value):
        return jnp.concatenate([-value[n_shot:], value[:n_shot]], 0)

    def one_slot(n, carry):
        name = slots[n, 0]
        there = jnp.where(name > 0, 1.0, 0.0)
        block = jnp.maximum(name - 1, 0)
        f = block // n_block
        b = block - f * n_block
        window = b // 2
        data = jnp.where(first_half, tiles[f, (window + 1) // 2], tiles[f, window // 2])
        lhs = jnp.concatenate([data, turned(data)], 1)
        raw = jnp.dot(lhs, table[f * 4 + b % 4], preferred_element_type=jnp.float32)
        beam_now = ((raw * cosine[f] + swapped(raw) * sine[f]) * there)
        at = pl.multiple_of(n * BR, BR)
        stacked[:, pl.ds(at, BR)] = beam_now.astype(jnp.bfloat16)
        stacked[:, pl.ds(pl.multiple_of(at + depth, BR), BR)] = turned(beam_now).astype(jnp.bfloat16)
        return carry

    lax.fori_loop(0, n_slot, one_slot, 0, unroll=8)

    for fetch in fetches[1:]:
        fetch.wait()

    def piece_copy(k, j):
        to = lax.rem(line + k, n_line)
        cols = pl.ds(j * CW, CW)
        return remote(
            part.at[to, :, cols], r_main.at[k - 1, :, cols], part_send.at[k - 1, j], part_recv.at[k - 1, j], to, tile
        )

    def edge_copy(k, up):
        to = lax.rem(line + k, n_line)
        if up:
            return remote(
                part.at[to, :, pl.ds(0, CW)], r_bot.at[k], top_send.at[k], bot_recv.at[k], to,
                jnp.maximum(tile - 1, 0),
            )
        return remote(
            part.at[to, :, pl.ds((pieces - 1) * CW, CW)], r_top.at[k], bot_send.at[k], top_recv.at[k], to,
            jnp.minimum(tile + 1, n_tile - 1),
        )

    for j in [0, pieces - 1, *range(1, pieces - 1)]:
        image = jnp.dot(stacked[...], beam[:, j * CW : (j + 1) * CW], preferred_element_type=jnp.float32)
        for to in range(n_line):
            low = to * shots
            part[to, :, j * CW : (j + 1) * CW] = jnp.concatenate(
                [image[low : low + shots], image[n_shot + low : n_shot + low + shots]], 0
            ).astype(jnp.bfloat16)
        if j == 0:

            @pl.when(tile > 0)
            def _():
                for k in range(n_line):
                    edge_copy(k, True).start()

        if j == pieces - 1:

            @pl.when(tile < n_tile - 1)
            def _():
                for k in range(n_line):
                    edge_copy(k, False).start()

        for k in range(1, n_line):
            piece_copy(k, j).start()

    @pl.when(line > 0)
    def _():
        head_out.wait_send()

    for c in meta_out:
        c.wait_send()
    for copy in (*mains, halo_copy):
        own(copy, lambda c: c.wait_send())
        for step, way in distances:
            onward(copy, step, way, lambda c: c.wait_send())

    @pl.when(tile > 0)
    def _():
        for k in range(n_line):
            edge_copy(k, False).wait_recv()
            edge_copy(k, True).wait_send()

    @pl.when(tile < n_tile - 1)
    def _():
        for k in range(n_line):
            edge_copy(k, True).wait_recv()
            edge_copy(k, False).wait_send()

    for j in range(pieces):
        for k in range(1, n_line):
            piece_copy(k, j).wait()

    wide = jnp.float32
    image_rows = []
    top = sum(r_top[k].astype(wide) for k in range(n_line))
    bottom = sum(r_bot[k].astype(wide) for k in range(n_line))
    image_rows += [top[:, :LANES], top[:, LANES:]]
    for row in range(out.shape[1]):
        cols = slice(row * LANES, (row + 1) * LANES)
        total = part[line, :, cols].astype(wide)
        for k in range(n_line - 1):
            total = total + r_main[k, :, cols].astype(wide)
        image_rows.append(total)
    image_rows += [bottom[:, :LANES], bottom[:, LANES:]]
    lane = lax.broadcasted_iota(jnp.int32, image_rows[0].shape, 1)
    for row in range(out.shape[1]):
        result = None
        for side in range(5):
            column = sum(dip[down, side] * image_rows[row + down] for down in range(5))
            move = side - 2
            if move:
                column = pltpu.roll(column, (-move) % LANES, 1)
                column = jnp.where((lane + move >= 0) & (lane + move < LANES), column, 0.0)
            result = column if result is None else result + column
        out[:, row, :] = result


def per_device(traces, codes, routes, beam_matrix, dip_filter):
    n_line, n_tile = lax.axis_size("line"), lax.axis_size("tile")
    n_shot = codes.shape[1]
    n_block = routes.shape[1]
    depth, pixels = beam_matrix.shape[3:]
    n_slot = depth // BR
    n_full = traces.shape[1] // LANES
    rows = 2 * (n_shot // n_line)
    tall = pixels // LANES
    pieces = pixels // CW
    table = jnp.asarray(slant_tables(n_tile)).astype(jnp.bfloat16)
    bf16, f32, i32 = jnp.bfloat16, jnp.float32, jnp.int32
    dma = pltpu.SemaphoreType.DMA
    vmem = pl.BlockSpec(memory_space=pltpu.VMEM)
    hbm = pl.BlockSpec(memory_space=pl.ANY)
    result = pl.pallas_call(
        functools.partial(kernel, n_line, n_tile, n_block, n_slot, n_shot),
        out_shape=jax.ShapeDtypeStruct((rows, tall, LANES), f32),
        in_specs=[hbm, vmem, vmem, pl.BlockSpec(memory_space=pltpu.SMEM), hbm, hbm],
        out_specs=vmem,
        scratch_shapes=[
            pltpu.VMEM(traces.shape[1:], bf16),
            pltpu.VMEM((n_tile, n_full + 1, LANES, LANES), bf16),
            pltpu.VMEM((n_tile, WIN // 2, LANES), bf16),
            pltpu.VMEM((n_tile, 8, LANES), i32),
            pltpu.VMEM(table.shape, bf16),
            pltpu.VMEM((2 * depth, pixels), bf16),
            pltpu.VMEM((n_slot, LANES), i32),
            pltpu.SMEM((n_slot, LANES), i32),
            pltpu.VMEM((n_tile, LANES, LANES), f32),
            pltpu.VMEM((n_tile, LANES, LANES), f32),
            pltpu.VMEM((2 * n_shot, 2 * depth), bf16),
            pltpu.VMEM((n_line, rows, pixels), bf16),
            pltpu.VMEM((n_line - 1, rows, pixels), bf16),
            pltpu.VMEM((n_line, rows, CW), bf16),
            pltpu.VMEM((n_line, rows, CW), bf16),
            dma((7,)),
            dma((2 * n_tile, 3)), dma((2 * n_tile,)),
            dma((n_tile, 3)), dma((n_tile,)),
            dma, dma,
            dma((n_tile,)), dma((n_tile,)),
            dma((n_line - 1, pieces)), dma((n_line - 1, pieces)),
            dma((n_line,)), dma((n_line,)),
            dma((n_line,)), dma((n_line,)),
        ],
        compiler_params=pltpu.CompilerParams(
            collective_id=0, has_side_effects=True, vmem_limit_bytes=60 * 2**20
        ),
    )(traces[0], codes, routes, dip_filter, table, beam_matrix.reshape(2 * depth, pixels))
    return result.reshape(2, rows // 2, tall, LANES)


def solution(mesh):
    in_specs = (
        P("tile", "line", None),
        P("tile", None),
        P("line", "tile"),
        P("line", "tile", None, None, None),
        P(),
    )
    out_specs = P(None, "line", "tile", None)
    return jax.shard_map(
        per_device, mesh=mesh, in_specs=in_specs, out_specs=out_specs, check_vma=False
    )
```
